512 devices in a mesh: chan: 32 (over x_hi, z, core), pair: 8 (over y), integ: 2 (over x_lo).
Axes of the slice: x: 4 (x_hi: 2, x_lo: 2; x = x_hi * 2 + x_lo), y: 8, z: 8, core: 2. Of those that a mesh axis runs over, the one named last changes fastest.
Arguments:
- spectra: bfloat16 [2, 32, 2048, 2048], P(None, None, ('chan', 'integ'), 'pair'), may hold values from -8 to 8
- pair_table: int32 [136, 2], P('pair'), may hold values from 0 to 15, as said below
Outputs:
- visibility: float32 [136, 32, 2, 128, 128], P('pair', 'chan', None, 'integ')
The draws below stay inside these ranges and needn't reach their ends.
Inputs may be any that keep to these rules, and one draw needn't show every extreme that they name: `pair_table`: each row names two antenna blocks a <= b (column 0 is a); every such pair of the 16 blocks stands in exactly one row.
All inputs are finite; a program needn't handle non-finite values.
Results may differ from the reference program's by a relative error of at most 0.0003.
Values may be sent and summed in bfloat16 or wider, within the bound.
No kernel may reach another device: no remote copies, remote signals or barrier semaphores. Data moves between devices by JAX's collectives and lax.ppermute only.
A program may use at most 64 MiB of HBM per device.

```python
import jax
import jax.numpy as jnp
import numpy as np
from jax import lax

INPUTS = 2048
BLOCK = 128
TIME = 2048
BLOCKS = 16
NPAIRS = 136
CHANNELS = 32


def draw_pair_table(key, part):
    key = jax.random.fold_in(key, 7)
    listing = np.array([[first, second] for first in range(BLOCKS) for second in range(first, BLOCKS)], dtype=np.int32)
    order = jax.random.permutation(key, NPAIRS)
    return jnp.asarray(listing)[order]


def block_scale(rng, extent, shards, smallest, largest):
    gain, own = 1.0, jax.random.fold_in(rng, 6)
    for position, shards_of in shards:
        steps = jnp.exp(jax.random.uniform(jax.random.fold_in(own, position), (shards_of,), jnp.float32, smallest / len(shards), largest / len(shards)))
        gain = gain * jnp.repeat(steps, extent[position] // shards_of).reshape([-1 if axis == position else 1 for axis in range(len(extent))])
    return gain


def centred(own_key, extent, width, most, cuts=(), held_as=jnp.bfloat16):
    entries = jax.random.normal(own_key, extent, jnp.float32) * width
    if len(cuts) > 0:
        entries = block_scale(own_key, extent, cuts, -0.22, 0.18) * entries
    return jnp.clip(entries, min=-most, max=most).astype(held_as)


def setup_inputs(seed: int = 0) -> dict:
    seeds = jax.random.split(jax.random.key(seed), 3)
    return {
        "spectra": centred(seeds[0], (2, CHANNELS, TIME, INPUTS), 2.0, 8.0, ((2, 64), (3, 8))),
        "pair_table": draw_pair_table(jax.random.fold_in(seeds[2], 71), 0),
    }


def reference(spectra, pair_table):
    def pair_tile(entry):
        first = (entry[0] * BLOCK).astype(jnp.int32)
        second = (entry[1] * BLOCK).astype(jnp.int32)
        left = lax.dynamic_slice_in_dim(spectra, first, BLOCK, 3).astype(jnp.float32)
        right = lax.dynamic_slice_in_dim(spectra, second, BLOCK, 3).astype(jnp.float32)
        high = lax.Precision.HIGHEST
        real_part = jnp.einsum("ctr,cts->crs", left[0], right[0], precision=high) + jnp.einsum("ctr,cts->crs", left[1], right[1], precision=high)
        imag_part = jnp.einsum("ctr,cts->crs", left[0], right[1], precision=high) - jnp.einsum("ctr,cts->crs", left[1], right[0], precision=high)
        return jnp.stack([real_part, imag_part], 1) * (1.0 / TIME)

    return lax.map(pair_tile, pair_table)
```

```python
import functools

import jax
import jax.numpy as jnp
from jax import lax
from jax.experimental import pallas as pl
from jax.experimental.pallas import tpu as pltpu
from jax.sharding import PartitionSpec as P

BLOCK = 128
TIME = 2048


def tiles_kernel(place, table, gathered, keep, send, whole):
    half = BLOCK // 2
    samples = gathered.shape[1] * gathered.shape[3]

    def both_parts(block):
        owner, lane = block // 2, pl.multiple_of(block % 2 * BLOCK, BLOCK)
        parts = [gathered[owner, :, i, :, pl.ds(lane, BLOCK)].reshape(samples, BLOCK) for i in range(2)]
        return jnp.concatenate(parts, axis=1)

    def tile(k, carry):
        left, right = both_parts(table[k, 0]), both_parts(table[k, 1])
        product = lax.dot_general(left, right, (((0,), (0,)), ((), ())), preferred_element_type=jnp.float32)
        whole[0] = product[:BLOCK, :BLOCK] + product[BLOCK:, BLOCK:]
        whole[1] = product[:BLOCK, BLOCK:] - product[BLOCK:, :BLOCK]
        keep[k] = whole[:, pl.ds(pl.multiple_of(place[0] * half, half), half), :]
        send[k] = whole[:, pl.ds(pl.multiple_of((1 - place[0]) * half, half), half), :]
        return carry

    lax.fori_loop(0, table.shape[0], tile, 0)


def tiles(place, table, gathered):
    count = table.shape[0]
    part = jax.ShapeDtypeStruct((count, 2, BLOCK // 2, BLOCK), jnp.float32)
    return pl.pallas_call(
        tiles_kernel,
        out_shape=(part, part),
        in_specs=[pl.BlockSpec(memory_space=pltpu.SMEM)] * 2 + [pl.BlockSpec(memory_space=pltpu.VMEM)],
        out_specs=(pl.BlockSpec(memory_space=pltpu.VMEM),) * 2,
        scratch_shapes=[pltpu.VMEM((2, BLOCK, BLOCK), jnp.float32)],
        compiler_params=pltpu.CompilerParams(vmem_limit_bytes=40 * 2**20),
        name="tiles",
    )(place, table, gathered)


def body(spectra, pair_table):
    by_channel = spectra.transpose(1, 0, 2, 3)
    turned = lax.all_to_all(by_channel, "chan", split_axis=0, concat_axis=0, tiled=True)
    gathered = lax.all_gather(turned, "pair", axis=0)
    place = lax.axis_index("integ")[None].astype(jnp.int32)
    keep, send = tiles(place, pair_table, gathered)
    other = lax.ppermute(send, "integ", [(0, 1), (1, 0)])
    return ((keep + other) * (1.0 / TIME))[:, None]


def solution(mesh):
    in_specs = (P(None, None, ("chan", "integ"), "pair"), P("pair", None))
    out_specs = P("pair", "chan", None, "integ", None)
    return jax.shard_map(body, mesh=mesh, in_specs=in_specs, out_specs=out_specs, check_vma=False)
```

```python
import jax
import jax.numpy as jnp
from jax import lax
from jax.experimental import pallas as pl
from jax.experimental.pallas import tpu as pltpu
from jax.sharding import PartitionSpec as P

BLOCK = 128
TIME = 2048
CHAINS = (11, 11, 10)
ROUND = [(c * 8 + y, c * 8 + (y + 1 - 2 * (c % 2)) % 8) for c in range(32) for y in range(8)]


def put_kernel(step, *refs):
    pieces, (held, token, arrived) = refs[-3 - len(CHAINS) : -3], refs[-3:]
    token[...] = jnp.zeros_like(token)
    copies, begin = [], 0
    for i, piece in enumerate(pieces):
        copies.append(pltpu.make_async_copy(piece, held.at[step, pl.ds(begin, piece.shape[0])], arrived.at[i]))
        begin += piece.shape[0]
    for copy in copies:
        copy.start()
    for copy in copies:
        copy.wait()


def put(step, held, token, pieces, early=()):
    sources = sum(piece.shape[0] for piece in pieces)
    operands = [*early, *pieces] if held is None else [held, token, *pieces]
    return pl.pallas_call(
        lambda *refs: put_kernel(step, *refs),
        out_shape=(
            jax.ShapeDtypeStruct((8, sources) + pieces[0].shape[1:], jnp.bfloat16),
            jax.ShapeDtypeStruct((8, 128), jnp.float32),
        ),
        in_specs=[pl.BlockSpec(memory_space=pltpu.SMEM)] * len(early)
        + [pl.BlockSpec(memory_space=pl.ANY)] * (len(operands) - len(early)),
        out_specs=(pl.BlockSpec(memory_space=pl.ANY), pl.BlockSpec(memory_space=pltpu.VMEM)),
        scratch_shapes=[pltpu.SemaphoreType.DMA((len(pieces),))],
        input_output_aliases={} if held is None else {0: 0},
        compiler_params=pltpu.CompilerParams(vmem_limit_bytes=2**20),
        cost_estimate=pl.CostEstimate(flops=0, bytes_accessed=2 * 2**20, transcendentals=0),
        name="put",
    )(*operands)


def rings(blocks, early):
    ends = [sum(CHAINS[:i]) for i in range(len(CHAINS) + 1)]
    now = [blocks[i:j] for i, j in zip(ends, ends[1:])]
    held = token = None
    for step in range(7):
        if held is not None:
            now[0], token = lax.optimization_barrier((now[0], token))
        passed = [lax.ppermute(piece, ("chan", "pair"), ROUND) for piece in now]
        (held, token), now = put(step, held, token, now, early if step == 0 else ()), passed
    return put(7, held, token, now)[0]


def tiles_kernel(where, table, held, keep, send, scale, whole):
    half = BLOCK // 2

    def columns(block):
        slot = lax.rem((block // 2 - where[0]) * where[2] + 8, 8)
        lane = pl.ds(pl.multiple_of(block % 2 * BLOCK, BLOCK), BLOCK)
        return jnp.concatenate([held[slot, :, i, :, lane].reshape(-1, BLOCK) for i in range(2)], axis=1)

    def tile(k, carry):
        left, right = columns(table[k, 0]), columns(table[k, 1])
        out = lax.dot_general(left, right, (((0,), (0,)), ((), ())), preferred_element_type=jnp.float32)
        whole[0] = (out[:BLOCK, :BLOCK] + out[BLOCK:, BLOCK:]) * (1.0 / TIME)
        whole[1] = (out[:BLOCK, BLOCK:] - out[BLOCK:, :BLOCK]) * (1.0 / TIME)
        keep[k] = whole[:, pl.ds(pl.multiple_of(where[1] * half, half), half), :]
        other = whole[:, pl.ds(pl.multiple_of((1 - where[1]) * half, half), half), :]
        most = jnp.max(jnp.abs(other), axis=1, keepdims=True)
        scale[k] = (most * (1.0 / 32767.0))[:, 0]
        send[k] = jnp.round(other * jnp.where(most > 0, 32767.0 / most, 0.0)).astype(jnp.int32).astype(jnp.int16)
        return carry

    lax.fori_loop(0, table.shape[0], tile, 0, unroll=True)


def tiles(where, table, held):
    count = table.shape[0]
    smem, vmem = (pl.BlockSpec(memory_space=s) for s in (pltpu.SMEM, pltpu.VMEM))
    part = jax.ShapeDtypeStruct((count, 2, BLOCK // 2, BLOCK), jnp.float32)
    return pl.pallas_call(
        tiles_kernel,
        out_shape=(
            part,
            jax.ShapeDtypeStruct(part.shape, jnp.int16),
            jax.ShapeDtypeStruct((count, 2, BLOCK), jnp.float32),
        ),
        in_specs=[smem, smem, vmem],
        out_specs=(vmem, vmem, vmem),
        scratch_shapes=[pltpu.VMEM((2, BLOCK, BLOCK), jnp.float32)],
        compiler_params=pltpu.CompilerParams(vmem_limit_bytes=4 * 2**20),
        cost_estimate=pl.CostEstimate(flops=count * 2 * 256 * 256 * 1024, bytes_accessed=10 * 2**20, transcendentals=0),
        name="tiles",
    )(where, table, held)


def body(spectra, pair_table):
    way = 2 * (lax.axis_index("chan") % 2) - 1
    where = jnp.stack([lax.axis_index("pair"), lax.axis_index("integ"), way]).astype(jnp.int32)
    turned = lax.all_to_all(spectra.transpose(1, 0, 2, 3), "chan", split_axis=0, concat_axis=0, tiled=True)
    keep, send, scale = tiles(where, pair_table, rings(turned, (where, pair_table)))
    send, scale = (lax.ppermute(half, "integ", [(0, 1), (1, 0)]) for half in (send, scale))
    return (keep + send.astype(jnp.float32) * scale[:, :, None])[:, None]


def solution(mesh):
    in_specs = (P(None, None, ("chan", "integ"), "pair"), P("pair", None))
    out_specs = P("pair", "chan", None, "integ", None)
    return jax.shard_map(body, mesh=mesh, in_specs=in_specs, out_specs=out_specs, check_vma=False)
```

```python
import jax
import jax.numpy as jnp
from jax import lax
from jax.experimental import pallas as pl
from jax.experimental.pallas import tpu as pltpu
from jax.sharding import PartitionSpec as P

BLOCK = 128
TIME = 2048
CHAINS = (11, 11, 10)
ROUND = [(c * 8 + y, c * 8 + (y + 1 - 2 * (c % 2)) % 8) for c in range(32) for y in range(8)]


def lay(step, pieces, held, arrived):
    copies, begin = [], 0
    for i, piece in enumerate(pieces):
        copies.append(pltpu.make_async_copy(piece, held.at[step, pl.ds(begin, piece.shape[0])], arrived.at[i]))
        begin += piece.shape[0]
    return copies


def run(copies):
    for copy in copies:
        copy.start()
    for copy in copies:
        copy.wait()


def put_kernel(steps, *refs):
    count = len(steps) * len(CHAINS)
    pieces, (held, token, arrived) = refs[-3 - count : -3], refs[-3:]
    token[...] = jnp.zeros_like(token)
    copies = []
    for i, step in enumerate(steps):
        here = pl.ds(len(CHAINS) * i, len(CHAINS))
        copies += lay(step, pieces[len(CHAINS) * i : len(CHAINS) * (i + 1)], held, arrived.at[here])
    run(copies)


def put(steps, held, token, pieces):
    sources = sum(piece.shape[0] for piece in pieces[: len(CHAINS)])
    operands = list(pieces) if held is None else [held, token, *pieces]
    return pl.pallas_call(
        lambda *refs: put_kernel(steps, *refs),
        out_shape=(
            jax.ShapeDtypeStruct((8, sources) + pieces[0].shape[1:], jnp.bfloat16),
            jax.ShapeDtypeStruct((8, 128), jnp.float32),
        ),
        in_specs=[pl.BlockSpec(memory_space=pl.ANY)] * len(operands),
        out_specs=(pl.BlockSpec(memory_space=pl.ANY), pl.BlockSpec(memory_space=pltpu.VMEM)),
        scratch_shapes=[pltpu.SemaphoreType.DMA((len(pieces),))],
        input_output_aliases={} if held is None else {0: 0},
        compiler_params=pltpu.CompilerParams(vmem_limit_bytes=2**20),
        cost_estimate=pl.CostEstimate(flops=0, bytes_accessed=2 * 2**20, transcendentals=0),
        name="put",
    )(*operands)


def rings(blocks):
    ends = [sum(CHAINS[:i]) for i in range(len(CHAINS) + 1)]
    now = [blocks[i:j] for i, j in zip(ends, ends[1:])]
    held = token = None
    first = now
    for step in range(7):
        if held is not None:
            now[0], token = lax.optimization_barrier((now[0], token))
        passed = [lax.ppermute(piece, ("chan", "pair"), ROUND) for piece in now]
        if step == 1:
            held, token = put((0, 1), None, None, first + now)
        elif step > 1:
            held, token = put((step,), held, token, now)
        now = passed
    return held, now


def products(where, table, held, sources, k):
    def columns(block):
        slot = lax.rem((block // 2 - where[0]) * where[2] + 8, 8)
        lane = pl.ds(pl.multiple_of(block % 2 * BLOCK, BLOCK), BLOCK)
        return jnp.concatenate([held[slot, sources, i, :, lane].reshape(-1, BLOCK) for i in range(2)], axis=1)

    left, right = columns(table[0, k]), columns(table[1, k])
    out = lax.dot_general(left, right, (((0,), (0,)), ((), ())), preferred_element_type=jnp.float32)
    return out[:BLOCK, :BLOCK] + out[BLOCK:, BLOCK:], out[:BLOCK, BLOCK:] - out[BLOCK:, :BLOCK]


def most_kernel(where, table, *refs):
    last, (held, total, arrived) = refs[1:-3], refs[-3:]
    run(lay(7, last, held, arrived))
    sources = pl.ds(0, sum(CHAINS[:-1]))

    def tile(k, carry):
        total[k, 0], total[k, 1] = products(where, table, held, sources, k)
        return carry

    lax.fori_loop(0, table.shape[1], tile, 0, unroll=True)


def rest_kernel(where, table, _, total, last, held, keep, send, scale, whole, arrived):
    half = BLOCK // 2
    sources = pl.ds(sum(CHAINS[:-1]), CHAINS[-1])
    run([pltpu.make_async_copy(last, held.at[7, sources], arrived)])

    def tile(k, carry):
        real, imag = products(where, table, held, sources, k)
        whole[0] = (total[k, 0] + real) * (1.0 / TIME)
        whole[1] = (total[k, 1] + imag) * (1.0 / TIME)
        keep[k] = whole[:, pl.ds(pl.multiple_of(where[1] * half, half), half), :]
        other = whole[:, pl.ds(pl.multiple_of((1 - where[1]) * half, half), half), :]
        most = jnp.max(jnp.abs(other), axis=1, keepdims=True)
        scale[k] = (most * (1.0 / 32767.0))[:, 0]
        send[k] = jnp.round(other * jnp.where(most > 0, 32767.0 / most, 0.0)).astype(jnp.int32).astype(jnp.int16)
        return carry

    lax.fori_loop(0, table.shape[1], tile, 0, unroll=True)


def tiles(where, table, held, last):
    count = table.shape[1]
    smem, vmem, any_ = (pl.BlockSpec(memory_space=s) for s in (pltpu.SMEM, pltpu.VMEM, pl.ANY))
    blocks = jax.ShapeDtypeStruct(held.shape, held.dtype)
    options = dict(
        compiler_params=pltpu.CompilerParams(vmem_limit_bytes=4 * 2**20),
        cost_estimate=pl.CostEstimate(flops=count * 256 * 256 * 1024, bytes_accessed=10 * 2**20, transcendentals=0),
        input_output_aliases={2: 0},
    )
    held, total = pl.pallas_call(
        most_kernel,
        out_shape=(blocks, jax.ShapeDtypeStruct((count, 2, BLOCK, BLOCK), jnp.float32)),
        in_specs=[smem, smem, vmem] + [any_] * (len(last) - 1),
        out_specs=(vmem, vmem),
        scratch_shapes=[pltpu.SemaphoreType.DMA((len(last) - 1,))],
        name="most",
        **options,
    )(where, table, held, *last[:-1])
    part = jax.ShapeDtypeStruct((count, 2, BLOCK // 2, BLOCK), jnp.float32)
    return pl.pallas_call(
        rest_kernel,
        out_shape=(
            blocks,
            part,
            jax.ShapeDtypeStruct(part.shape, jnp.int16),
            jax.ShapeDtypeStruct((count, 2, BLOCK), jnp.float32),
        ),
        in_specs=[smem, smem, vmem, vmem, any_],
        out_specs=(vmem, vmem, vmem, vmem),
        scratch_shapes=[pltpu.VMEM((2, BLOCK, BLOCK), jnp.float32), pltpu.SemaphoreType.DMA],
        name="rest",
        **options,
    )(where, table, held, total, last[-1])


def body(spectra, pair_table):
    way = 2 * (lax.axis_index("chan") % 2) - 1
    where = jnp.stack([lax.axis_index("pair"), lax.axis_index("integ"), way]).astype(jnp.int32)
    ordered, where, table = lax.optimization_barrier((spectra.transpose(1, 0, 2, 3), where, pair_table.T))
    turned = lax.all_to_all(ordered, "chan", split_axis=0, concat_axis=0, tiled=True)
    _, keep, send, scale = tiles(where, table, *rings(turned))
    send, scale = (lax.ppermute(half, "integ", [(0, 1), (1, 0)]) for half in (send, scale))
    return (keep + send.astype(jnp.float32) * scale[:, :, None])[:, None]


def solution(mesh):
    in_specs = (P(None, None, ("chan", "integ"), "pair"), P("pair", None))
    out_specs = P("pair", "chan", None, "integ", None)
    return jax.shard_map(body, mesh=mesh, in_specs=in_specs, out_specs=out_specs, check_vma=False)
```

```python
import jax
import jax.numpy as jnp
from jax import lax
from jax.experimental import pallas as pl
from jax.experimental.pallas import tpu as pltpu
from jax.sharding import PartitionSpec as P

BLOCK = 128
TIME = 2048
STEPS = 32767.0
CHAINS = (11, 11, 10)
ROUND = [(c * 8 + y, c * 8 + (y + 1 - 2 * (c % 2)) % 8) for c in range(32) for y in range(8)]


def lay(step, pieces, held, arrived):
    copies, begin = [], 0
    for i, piece in enumerate(pieces):
        copies.append(pltpu.make_async_copy(piece, held.at[step, pl.ds(begin, piece.shape[0])], arrived.at[i]))
        begin += piece.shape[0]
    return copies


def run(copies):
    for copy in copies:
        copy.start()
    for copy in copies:
        copy.wait()


def put_kernel(steps, *refs):
    count = len(steps) * len(CHAINS)
    pieces, (held, token, arrived) = refs[-3 - count : -3], refs[-3:]
    token[...] = jnp.zeros_like(token)
    copies = []
    for i, step in enumerate(steps):
        here = pl.ds(len(CHAINS) * i, len(CHAINS))
        copies += lay(step, pieces[len(CHAINS) * i : len(CHAINS) * (i + 1)], held, arrived.at[here])
    run(copies)


def put(steps, held, token, pieces):
    sources = sum(piece.shape[0] for piece in pieces[: len(CHAINS)])
    operands = list(pieces) if held is None else [held, token, *pieces]
    return pl.pallas_call(
        lambda *refs: put_kernel(steps, *refs),
        out_shape=(
            jax.ShapeDtypeStruct((8, sources) + pieces[0].shape[1:], jnp.bfloat16),
            jax.ShapeDtypeStruct((8, 128), jnp.float32),
        ),
        in_specs=[pl.BlockSpec(memory_space=pl.ANY)] * len(operands),
        out_specs=(pl.BlockSpec(memory_space=pl.ANY), pl.BlockSpec(memory_space=pltpu.VMEM)),
        scratch_shapes=[pltpu.SemaphoreType.DMA((len(pieces),))],
        input_output_aliases={} if held is None else {0: 0},
        compiler_params=pltpu.CompilerParams(vmem_limit_bytes=2**20),
        cost_estimate=pl.CostEstimate(flops=0, bytes_accessed=2 * 2**20, transcendentals=0),
        name="put",
    )(*operands)


def rings(blocks):
    ends = [sum(CHAINS[:i]) for i in range(len(CHAINS) + 1)]
    now = [blocks[i:j] for i, j in zip(ends, ends[1:])]
    held = token = None
    first = now
    for step in range(7):
        if held is not None:
            now[0], token = lax.optimization_barrier((now[0], token))
        passed = [lax.ppermute(piece, ("chan", "pair"), ROUND) for piece in now]
        if step == 1:
            held, token = put((0, 1), None, None, first + now)
        elif step > 1:
            held, token = put((step,), held, token, now)
        now = passed
    return held, now


def products(where, table, held, sources, k):
    def columns(block):
        slot = lax.rem((block // 2 - where[0]) * where[2] + 8, 8)
        lane = pl.ds(pl.multiple_of(block % 2 * BLOCK, BLOCK), BLOCK)
        return jnp.concatenate([held[slot, sources, i, :, lane].reshape(-1, BLOCK) for i in range(2)], axis=1)

    left, right = columns(table[0, k]), columns(table[1, k])
    out = lax.dot_general(left, right, (((0,), (0,)), ((), ())), preferred_element_type=jnp.float32)
    return out[:BLOCK, :BLOCK] + out[BLOCK:, BLOCK:], out[:BLOCK, BLOCK:] - out[BLOCK:, :BLOCK]


def most_kernel(where, table, *refs):
    last, (held, total, arrived) = refs[1:-3], refs[-3:]
    run(lay(7, last, held, arrived))
    sources = pl.ds(0, sum(CHAINS[:-1]))

    def tile(k, carry):
        total[k, 0], total[k, 1] = products(where, table, held, sources, k)
        return carry

    lax.fori_loop(0, table.shape[1], tile, 0, unroll=True)


def rest_kernel(where, table, _, total, last, held, keep, send, scale, whole, arrived):
    half = BLOCK // 2
    sources = pl.ds(sum(CHAINS[:-1]), CHAINS[-1])
    run([pltpu.make_async_copy(last, held.at[7, sources], arrived)])

    def tile(k, carry):
        real, imag = products(where, table, held, sources, k)
        whole[0] = (total[k, 0] + real) * (1.0 / TIME)
        whole[1] = (total[k, 1] + imag) * (1.0 / TIME)
        keep[k] = whole[:, pl.ds(pl.multiple_of(where[1] * half, half), half), :]
        other = whole[:, pl.ds(pl.multiple_of((1 - where[1]) * half, half), half), :]
        most = jnp.max(jnp.abs(other), axis=1, keepdims=True)
        scale[k] = most[:, 0]
        send[k] = jnp.round(other * jnp.where(most > 0, 1.0 / most, 0.0) * STEPS).astype(jnp.int32).astype(jnp.int16)
        return carry

    lax.fori_loop(0, table.shape[1], tile, 0, unroll=True)


def tiles(where, table, held, last):
    count = table.shape[1]
    smem, vmem, any_ = (pl.BlockSpec(memory_space=s) for s in (pltpu.SMEM, pltpu.VMEM, pl.ANY))
    blocks = jax.ShapeDtypeStruct(held.shape, held.dtype)
    options = dict(
        compiler_params=pltpu.CompilerParams(vmem_limit_bytes=4 * 2**20),
        cost_estimate=pl.CostEstimate(flops=count * 256 * 256 * 1024, bytes_accessed=10 * 2**20, transcendentals=0),
        input_output_aliases={2: 0},
    )
    held, total = pl.pallas_call(
        most_kernel,
        out_shape=(blocks, jax.ShapeDtypeStruct((count, 2, BLOCK, BLOCK), jnp.float32)),
        in_specs=[smem, smem, vmem] + [any_] * (len(last) - 1),
        out_specs=(vmem, vmem),
        scratch_shapes=[pltpu.SemaphoreType.DMA((len(last) - 1,))],
        name="most",
        **options,
    )(where, table, held, *last[:-1])
    part = jax.ShapeDtypeStruct((count, 2, BLOCK // 2, BLOCK), jnp.float32)
    return pl.pallas_call(
        rest_kernel,
        out_shape=(
            blocks,
            part,
            jax.ShapeDtypeStruct(part.shape, jnp.int16),
            jax.ShapeDtypeStruct((count, 2, BLOCK), jnp.float32),
        ),
        in_specs=[smem, smem, vmem, vmem, any_],
        out_specs=(vmem, vmem, vmem, vmem),
        scratch_shapes=[pltpu.VMEM((2, BLOCK, BLOCK), jnp.float32), pltpu.SemaphoreType.DMA],
        name="rest",
        **options,
    )(where, table, held, total, last[-1])


def body(spectra, pair_table):
    way = 2 * (lax.axis_index("chan") % 2) - 1
    where = jnp.stack([lax.axis_index("pair"), lax.axis_index("integ"), way]).astype(jnp.int32)
    ordered, where, table = lax.optimization_barrier((spectra.transpose(1, 0, 2, 3), where, pair_table.T))
    turned = lax.all_to_all(ordered, "chan", split_axis=0, concat_axis=0, tiled=True)
    _, keep, send, scale = tiles(where, table, *rings(turned))
    send, scale = (lax.ppermute(half, "integ", [(0, 1), (1, 0)]) for half in (send, scale))
    return (keep + send.astype(jnp.float32) * (1.0 / STEPS) * scale[:, :, None])[:, None]


def solution(mesh):
    in_specs = (P(None, None, ("chan", "integ"), "pair"), P("pair", None))
    out_specs = P("pair", "chan", None, "integ", None)
    return jax.shard_map(body, mesh=mesh, in_specs=in_specs, out_specs=out_specs, check_vma=False)
```

```python
import jax
import jax.numpy as jnp
from jax import lax
from jax.experimental import pallas as pl
from jax.experimental.pallas import tpu as pltpu
from jax.sharding import PartitionSpec as P

BLOCK = 128
TIME = 2048
STEPS = 32767.0
CHAINS = (11, 11, 10)
ROUND = [(c * 8 + y, c * 8 + (y + 1 - 2 * (c % 2)) % 8) for c in range(32) for y in range(8)]


def lay(step, pieces, held, arrived):
    copies, begin = [], 0
    for i, piece in enumerate(pieces):
        copies.append(pltpu.make_async_copy(piece, held.at[step, pl.ds(begin, piece.shape[0])], arrived.at[i]))
        begin += piece.shape[0]
    return copies


def run(copies):
    for copy in copies:
        copy.start()
    for copy in copies:
        copy.wait()


def put_kernel(steps, *refs):
    count = len(steps) * len(CHAINS)
    pieces, (held, token, arrived) = refs[-3 - count : -3], refs[-3:]
    token[...] = jnp.zeros_like(token)
    copies = []
    for i, step in enumerate(steps):
        here = pl.ds(len(CHAINS) * i, len(CHAINS))
        copies += lay(step, pieces[len(CHAINS) * i : len(CHAINS) * (i + 1)], held, arrived.at[here])
    run(copies)


def put(steps, held, token, pieces):
    sources = sum(piece.shape[0] for piece in pieces[: len(CHAINS)])
    operands = list(pieces) if held is None else [held, token, *pieces]
    return pl.pallas_call(
        lambda *refs: put_kernel(steps, *refs),
        out_shape=(
            jax.ShapeDtypeStruct((8, sources) + pieces[0].shape[1:], jnp.bfloat16),
            jax.ShapeDtypeStruct((8, 128), jnp.float32),
        ),
        in_specs=[pl.BlockSpec(memory_space=pl.ANY)] * len(operands),
        out_specs=(pl.BlockSpec(memory_space=pl.ANY), pl.BlockSpec(memory_space=pltpu.VMEM)),
        scratch_shapes=[pltpu.SemaphoreType.DMA((len(pieces),))],
        input_output_aliases={} if held is None else {0: 0},
        compiler_params=pltpu.CompilerParams(vmem_limit_bytes=2**20),
        cost_estimate=pl.CostEstimate(flops=0, bytes_accessed=2 * 2**20, transcendentals=0),
        name="put",
    )(*operands)


def rings(blocks):
    ends = [sum(CHAINS[:i]) for i in range(len(CHAINS) + 1)]
    now = [blocks[i:j] for i, j in zip(ends, ends[1:])]
    held = token = None
    first = now
    for step in range(7):
        if held is not None:
            now[0], token = lax.optimization_barrier((now[0], token))
        passed = [lax.ppermute(piece, ("chan", "pair"), ROUND) for piece in now]
        if step == 1:
            held, token = put((0, 1), None, None, first + now)
        elif step > 1:
            held, token = put((step,), held, token, now)
        now = passed
    return held, now


def products(where, table, held, sources, k):
    def columns(block):
        slot = lax.rem((block // 2 - where[0]) * where[2] + 8, 8)
        lane = pl.ds(pl.multiple_of(block % 2 * BLOCK, BLOCK), BLOCK)
        return jnp.concatenate([held[slot, sources, i, :, lane].reshape(-1, BLOCK) for i in range(2)], axis=1)

    left, right = columns(table[0, k]), columns(table[1, k])
    out = lax.dot_general(left, right, (((0,), (0,)), ((), ())), preferred_element_type=jnp.float32)
    return out[:BLOCK, :BLOCK] + out[BLOCK:, BLOCK:], out[:BLOCK, BLOCK:] - out[BLOCK:, :BLOCK]


def most_kernel(where, table, *refs):
    last, (held, total, arrived) = refs[1:-3], refs[-3:]
    run(lay(7, last, held, arrived))
    sources = pl.ds(0, sum(CHAINS[:-1]))

    def tile(k, carry):
        total[k, 0], total[k, 1] = products(where, table, held, sources, k)
        return carry

    lax.fori_loop(0, table.shape[1], tile, 0, unroll=True)


def rest_kernel(where, table, _, total, last, held, keep, send, scale):
    half = BLOCK // 2
    sources = pl.ds(sum(CHAINS[:-1]), CHAINS[-1])
    held[7, sources] = last[...]

    def tile(k, carry):
        real, imag = products(where, table, held, sources, k)
        parts = [(total[k, i] + part) * (1.0 / TIME) for i, part in enumerate((real, imag))]
        top = jnp.stack([part[:half] for part in parts])
        bottom = jnp.stack([part[half:] for part in parts])
        mine_is_top = where[1] == 0
        keep[k] = jnp.where(mine_is_top, top, bottom)
        other = jnp.where(mine_is_top, bottom, top)
        most = jnp.max(jnp.abs(other), axis=1, keepdims=True)
        scale[k] = most[:, 0]
        send[k] = jnp.round(other * jnp.where(most > 0, 1.0 / most, 0.0) * STEPS).astype(jnp.int32).astype(jnp.int16)
        return carry

    lax.fori_loop(0, table.shape[1], tile, 0, unroll=True)


def tiles(where, table, held, last):
    count = table.shape[1]
    smem, vmem, any_ = (pl.BlockSpec(memory_space=s) for s in (pltpu.SMEM, pltpu.VMEM, pl.ANY))
    blocks = jax.ShapeDtypeStruct(held.shape, held.dtype)
    options = dict(
        compiler_params=pltpu.CompilerParams(vmem_limit_bytes=4 * 2**20),
        cost_estimate=pl.CostEstimate(flops=count * 256 * 256 * 1024, bytes_accessed=10 * 2**20, transcendentals=0),
        input_output_aliases={2: 0},
    )
    held, total = pl.pallas_call(
        most_kernel,
        out_shape=(blocks, jax.ShapeDtypeStruct((count, 2, BLOCK, BLOCK), jnp.float32)),
        in_specs=[smem, smem, vmem] + [any_] * (len(last) - 1),
        out_specs=(vmem, vmem),
        scratch_shapes=[pltpu.SemaphoreType.DMA((len(last) - 1,))],
        name="most",
        **options,
    )(where, table, held, *last[:-1])
    part = jax.ShapeDtypeStruct((count, 2, BLOCK // 2, BLOCK), jnp.float32)
    return pl.pallas_call(
        rest_kernel,
        out_shape=(
            blocks,
            part,
            jax.ShapeDtypeStruct(part.shape, jnp.int16),
            jax.ShapeDtypeStruct((count, 2, BLOCK), jnp.float32),
        ),
        in_specs=[smem, smem, vmem, vmem, vmem],
        out_specs=(vmem, vmem, vmem, vmem),
        name="rest",
        **options,
    )(where, table, held, total, last[-1])


def body(spectra, pair_table):
    way = 2 * (lax.axis_index("chan") % 2) - 1
    where = jnp.stack([lax.axis_index("pair"), lax.axis_index("integ"), way]).astype(jnp.int32)
    ordered, where, table = lax.optimization_barrier((spectra.transpose(1, 0, 2, 3), where, pair_table.T))
    turned = lax.all_to_all(ordered, "chan", split_axis=0, concat_axis=0, tiled=True)
    _, keep, send, scale = tiles(where, table, *rings(turned))
    send, scale = (lax.ppermute(half, "integ", [(0, 1), (1, 0)]) for half in (send, scale))
    return (keep + send.astype(jnp.float32) * (1.0 / STEPS) * scale[:, :, None])[:, None]


def solution(mesh):
    in_specs = (P(None, None, ("chan", "integ"), "pair"), P("pair", None))
    out_specs = P("pair", "chan", None, "integ", None)
    return jax.shard_map(body, mesh=mesh, in_specs=in_specs, out_specs=out_specs, check_vma=False)
```

```python
import jax
import jax.numpy as jnp
from jax import lax
from jax.experimental import pallas as pl
from jax.experimental.pallas import tpu as pltpu
from jax.sharding import PartitionSpec as P

BLOCK = 128
TIME = 2048
STEPS = 32767.0
CHAINS = (11, 11, 10)
ROUND = [(c * 8 + y, c * 8 + (y + 1 - 2 * (c % 2)) % 8) for c in range(32) for y in range(8)]


def lay(step, pieces, held, arrived):
    copies, begin = [], 0
    for i, piece in enumerate(pieces):
        copies.append(pltpu.make_async_copy(piece, held.at[step, pl.ds(begin, piece.shape[0])], arrived.at[i]))
        begin += piece.shape[0]
    return copies


def run(copies):
    for copy in copies:
        copy.start()
    for copy in copies:
        copy.wait()


def put_kernel(steps, *refs):
    count = len(steps) * len(CHAINS)
    pieces, (held, token, arrived) = refs[-3 - count : -3], refs[-3:]
    token[...] = jnp.zeros_like(token)
    copies = []
    for i, step in enumerate(steps):
        here = pl.ds(len(CHAINS) * i, len(CHAINS))
        copies += lay(step, pieces[len(CHAINS) * i : len(CHAINS) * (i + 1)], held, arrived.at[here])
    run(copies)


def put(steps, held, token, pieces):
    sources = sum(piece.shape[0] for piece in pieces[: len(CHAINS)])
    operands = list(pieces) if held is None else [held, token, *pieces]
    return pl.pallas_call(
        lambda *refs: put_kernel(steps, *refs),
        out_shape=(
            jax.ShapeDtypeStruct((8, sources) + pieces[0].shape[1:], jnp.bfloat16),
            jax.ShapeDtypeStruct((8, 128), jnp.float32),
        ),
        in_specs=[pl.BlockSpec(memory_space=pl.ANY)] * len(operands),
        out_specs=(pl.BlockSpec(memory_space=pl.ANY), pl.BlockSpec(memory_space=pltpu.VMEM)),
        scratch_shapes=[pltpu.SemaphoreType.DMA((len(pieces),))],
        input_output_aliases={} if held is None else {0: 0},
        compiler_params=pltpu.CompilerParams(vmem_limit_bytes=2**20),
        cost_estimate=pl.CostEstimate(flops=0, bytes_accessed=2 * 2**20, transcendentals=0),
        name="put",
    )(*operands)


def rings(blocks):
    ends = [sum(CHAINS[:i]) for i in range(len(CHAINS) + 1)]
    now = [blocks[i:j] for i, j in zip(ends, ends[1:])]
    held = token = None
    first = now
    for step in range(7):
        if held is not None:
            now[0], token = lax.optimization_barrier((now[0], token))
        passed = [lax.ppermute(piece, ("chan", "pair"), ROUND) for piece in now]
        if step == 1:
            held, token = put((0, 1), None, None, first + now)
        elif step > 1:
            held, token = put((step,), held, token, now)
        now = passed
    return held, now


def products(where, table, held, sources, k):
    def columns(block):
        slot = lax.rem((block // 2 - where[0]) * where[2] + 8, 8)
        lane = pl.ds(pl.multiple_of(block % 2 * BLOCK, BLOCK), BLOCK)
        return jnp.concatenate([held[slot, sources, i, :, lane].reshape(-1, BLOCK) for i in range(2)], axis=1)

    left, right = columns(table[0, k]), columns(table[1, k])
    out = lax.dot_general(left, right, (((0,), (0,)), ((), ())), preferred_element_type=jnp.float32)
    return out[:BLOCK, :BLOCK] + out[BLOCK:, BLOCK:], out[:BLOCK, BLOCK:] - out[BLOCK:, :BLOCK]


def most_kernel(where, table, *refs):
    last, (held, total, arrived) = refs[1:-3], refs[-3:]
    run(lay(7, last, held, arrived))
    sources = pl.ds(0, sum(CHAINS[:-1]))

    def tile(k, carry):
        total[k, 0], total[k, 1] = products(where, table, held, sources, k)
        return carry

    lax.fori_loop(0, table.shape[1], tile, 0, unroll=True)


def rest_kernel(where, table, _, total, last, held, keep, send, scale, whole, arrived):
    half = BLOCK // 2
    sources = pl.ds(sum(CHAINS[:-1]), CHAINS[-1])
    run([pltpu.make_async_copy(last, held.at[7, sources], arrived)])

    def tile(k, carry):
        real, imag = products(where, table, held, sources, k)
        whole[0] = total[k, 0] + real
        whole[1] = total[k, 1] + imag
        keep[k] = whole[:, pl.ds(pl.multiple_of(where[1] * half, half), half), :]
        other = whole[:, pl.ds(pl.multiple_of((1 - where[1]) * half, half), half), :]
        most = jnp.max(jnp.abs(other), axis=1, keepdims=True)
        scale[k] = most[:, 0]
        send[k] = jnp.round(other * jnp.where(most > 0, 1.0 / most, 0.0) * STEPS).astype(jnp.int32).astype(jnp.int16)
        return carry

    lax.fori_loop(0, table.shape[1], tile, 0, unroll=True)


def tiles(where, table, held, last):
    count = table.shape[1]
    smem, vmem, any_ = (pl.BlockSpec(memory_space=s) for s in (pltpu.SMEM, pltpu.VMEM, pl.ANY))
    blocks = jax.ShapeDtypeStruct(held.shape, held.dtype)
    options = dict(
        compiler_params=pltpu.CompilerParams(vmem_limit_bytes=4 * 2**20),
        cost_estimate=pl.CostEstimate(flops=count * 256 * 256 * 1024, bytes_accessed=10 * 2**20, transcendentals=0),
        input_output_aliases={2: 0},
    )
    held, total = pl.pallas_call(
        most_kernel,
        out_shape=(blocks, jax.ShapeDtypeStruct((count, 2, BLOCK, BLOCK), jnp.float32)),
        in_specs=[smem, smem, vmem] + [any_] * (len(last) - 1),
        out_specs=(vmem, vmem),
        scratch_shapes=[pltpu.SemaphoreType.DMA((len(last) - 1,))],
        name="most",
        **options,
    )(where, table, held, *last[:-1])
    part = jax.ShapeDtypeStruct((count, 2, BLOCK // 2, BLOCK), jnp.float32)
    return pl.pallas_call(
        rest_kernel,
        out_shape=(
            blocks,
            part,
            jax.ShapeDtypeStruct(part.shape, jnp.int16),
            jax.ShapeDtypeStruct((count, 2, BLOCK), jnp.float32),
        ),
        in_specs=[smem, smem, vmem, vmem, any_],
        out_specs=(vmem, vmem, vmem, vmem),
        scratch_shapes=[pltpu.VMEM((2, BLOCK, BLOCK), jnp.float32), pltpu.SemaphoreType.DMA],
        name="rest",
        **options,
    )(where, table, held, total, last[-1])


def body(spectra, pair_table):
    way = 2 * (lax.axis_index("chan") % 2) - 1
    where = jnp.stack([lax.axis_index("pair"), lax.axis_index("integ"), way]).astype(jnp.int32)
    ordered, where, table = lax.optimization_barrier((spectra.transpose(1, 0, 2, 3), where, pair_table.T))
    turned = lax.all_to_all(ordered, "chan", split_axis=0, concat_axis=0, tiled=True)
    _, keep, send, scale = tiles(where, table, *rings(turned))
    send, scale = (lax.ppermute(half, "integ", [(0, 1), (1, 0)]) for half in (send, scale))
    return ((keep + send.astype(jnp.float32) * (1.0 / STEPS) * scale[:, :, None]) * (1.0 / TIME))[:, None]


def solution(mesh):
    in_specs = (P(None, None, ("chan", "integ"), "pair"), P("pair", None))
    out_specs = P("pair", "chan", None, "integ", None)
    return jax.shard_map(body, mesh=mesh, in_specs=in_specs, out_specs=out_specs, check_vma=False)
```
